32 devices in a mesh: parts: 2 (over x), blocks: 16 (over z, y, core).
Axes of the slice: x: 2, y: 2, z: 4, core: 2. Of those that a mesh axis runs over, the one named last changes fastest.
Arguments:
- coords: float32 [640, 3, 32768], P('blocks', None, 'parts'), parts along dimension 2
- pairs: int32 [2, 2048], replicated, may hold values from 0 to 639
- res_slot: int32 [640], replicated, may hold values from 0 to 639, each once
Outputs:
- distances: bfloat16 [4, 32768, 1024], P(None, ('parts', 'blocks')), parts along dimension 1
The draws below stay inside these ranges and needn't reach their ends.
There are 2 independent parts, one for each index of `parts`. The reference program is written for one: setup_inputs(seed, part) draws one part's arguments, and reference() takes and returns one part's arrays. A program takes and returns all parts, laid end to end along the dimension named above; an argument that names none is the same for every part. Nothing has to cross between parts.
All inputs are finite; a program needn't handle non-finite values.
Results may differ from the reference program's by a relative error of at most 0.0025.
Values may be sent and summed in bfloat16 or wider, within the bound.
A program may use at most 192 MiB of HBM per device.

```python
import math
import jax
import jax.numpy as jnp
from jax import lax

RESIDUES = 640
CONTACTS = 2048
FB = 1024
ROUNDS = 4
FRAMES = 16384
N_BLOCKS = 16


def draw_coords(key, part):
    key_base, key_amp, key_noise = jax.random.split(jax.random.fold_in(key, 11), 3)
    base = 4.0 * jax.random.normal(key_base, (RESIDUES, 3, 1), jnp.float32)
    amplitude = jnp.exp(jax.random.uniform(key_amp, (1, 1, FRAMES), jnp.float32, math.log(0.4), math.log(5.0)))
    noise = jax.random.normal(key_noise, (RESIDUES, 3, FRAMES), jnp.float32)
    breath = jnp.ones((1, 1, FRAMES), jnp.float32)
    return base * breath + amplitude * noise


def with_ends(drawn, own_key, low, top_value):
    shape = drawn.shape
    place = [jax.random.randint(jax.random.fold_in(own_key, axis), (), 0, shape[axis]) for axis in range(len(shape))]
    drawn = drawn.at[tuple(place)].set(low)
    longest = shape.index(max(shape))
    place[longest] = (place[longest] + 1) % shape[longest]
    return drawn.at[tuple(place)].set(top_value)


def setup_inputs(seed: int = 0, part: int = 0) -> dict:
    arg_keys = jax.random.split(jax.random.key(seed), 4)
    part_keys = jax.random.split(jax.random.fold_in(arg_keys[3], part), 4)
    coords = draw_coords(jax.random.fold_in(jax.random.fold_in(arg_keys[3], part), 71), part)
    pairs = with_ends(jax.random.randint(arg_keys[1], (2, CONTACTS), 0, RESIDUES), jax.random.fold_in(arg_keys[1], 1), 0, RESIDUES - 1).astype(jnp.int32)
    res_slot = jax.random.permutation(arg_keys[2], RESIDUES).astype(jnp.int32)
    return dict(coords=coords, pairs=pairs, res_slot=res_slot)


def featurize(block, slot_first, slot_second):
    squared = jnp.zeros((slot_first.shape[0], block.shape[2]), jnp.float32)
    for component in range(3):
        offset = block[slot_first, component] - block[slot_second, component]
        squared = squared + offset * offset
    separation = jnp.sqrt(squared + 0.01)
    return jax.nn.sigmoid((8.0 - separation) / 1.5).T.astype(jnp.bfloat16)

def reference(coords, pairs, res_slot):
    position = jnp.zeros((RESIDUES,), jnp.int32).at[res_slot].set(jnp.arange(RESIDUES, dtype=jnp.int32))
    slot_first = position[pairs[0]]
    slot_second = position[pairs[1]]
    grouped = coords.reshape(RESIDUES, 3, N_BLOCKS, FB).transpose(2, 0, 1, 3)
    features = lax.map(lambda block: featurize(block, slot_first, slot_second), grouped)
    wide = features.astype(jnp.float32)
    norms = lax.optimization_barrier(jnp.sum(wide * wide, axis=-1))

    def tanimoto(items):
        own, visitor, own_norm, vis_norm = items
        intersection = jnp.dot(own, visitor.T, preferred_element_type=jnp.float32)
        ratio = intersection / (own_norm[:, None] + vis_norm[None, :] - intersection + 1e-06)
        return (1.0 - ratio).astype(jnp.bfloat16)
    results = []
    for offset_round in range(1, ROUNDS + 1):
        visitors = jnp.roll(features, offset_round, axis=0)
        vis_norms = jnp.roll(norms, offset_round, axis=0)
        block_dist = lax.map(tanimoto, (features, visitors, norms, vis_norms))
        results.append(block_dist.reshape(FRAMES, FB))
    return jnp.stack(results)
```

```python
import functools
import jax
import jax.numpy as jnp
from jax import lax
from jax.experimental import pallas as pl
from jax.experimental.pallas import tpu as pltpu
from jax.sharding import PartitionSpec as P

ROUNDS = 4
LANES = 128
TOP_CODE = 32767.0
MESH = pl.DeviceIdType.MESH


def encode_kernel(x_ref, code_ref, meta_ref, tmp, params):
    _, res, frames = x_ref.shape
    rows = frames // LANES
    half = None
    centers = []
    for k in range(3):
        x = x_ref[k]
        top = jnp.max(x, axis=0, keepdims=True)
        low = jnp.min(x, axis=0, keepdims=True)
        center = (0.5 * top + 0.5 * low).astype(jnp.bfloat16).astype(jnp.float32)
        reach = jnp.maximum(top - center, center - low)
        half = reach if half is None else jnp.maximum(half, reach)
        centers.append(center)
    step = jnp.maximum(half * (1.01 / TOP_CODE), 1e-30).astype(jnp.bfloat16).astype(jnp.float32)
    inverse = 1.0 / step
    for k in range(3):
        scaled = jnp.round((x_ref[k] - centers[k]) * inverse)
        for s in range(rows):
            tmp[pl.ds(s, res, stride=rows), :] = scaled[:, s * LANES:(s + 1) * LANES]
        code_ref[0, k] = tmp[...].astype(jnp.int32).astype(jnp.int16)
    for k, plane in enumerate(centers + [step]):
        for s in range(rows):
            params[k * rows + s:k * rows + s + 1, :] = plane[:, s * LANES:(s + 1) * LANES]
    meta_ref[0] = params[...].astype(jnp.bfloat16)


def encode(coords, blocks):
    _, res, frames = coords.shape
    per_block = frames // blocks
    rows = per_block // LANES
    return pl.pallas_call(
        encode_kernel,
        grid=(blocks,),
        in_specs=[pl.BlockSpec((3, res, per_block), lambda d: (0, 0, d))],
        out_specs=[
            pl.BlockSpec((1, 3, res * rows, LANES), lambda d: (d, 0, 0, 0)),
            pl.BlockSpec((1, 4 * rows, LANES), lambda d: (d, 0, 0)),
        ],
        out_shape=[
            jax.ShapeDtypeStruct((blocks, 3, res * rows, LANES), jnp.int16),
            jax.ShapeDtypeStruct((blocks, 4 * rows, LANES), jnp.bfloat16),
        ],
        scratch_shapes=[
            pltpu.VMEM((res * rows, LANES), jnp.float32),
            pltpu.VMEM((4 * rows, LANES), jnp.float32),
        ],
        compiler_params=pltpu.CompilerParams(vmem_limit_bytes=32 * 2**20),
    )(coords)


def feature_kernel(first_ref, second_ref, code_ref, meta_ref, out_ref, grid_ref, tmp):
    blocks, _, span, _ = code_ref.shape
    rows = meta_ref.shape[1] // 4
    contacts = out_ref.shape[0]

    def decode(b, carry):
        meta = meta_ref[b].astype(jnp.float32)
        step = meta[3 * rows:4 * rows][None]
        for k in range(3):
            code = code_ref[b, k].astype(jnp.int32).astype(jnp.float32)
            value = code.reshape(span // rows, rows, LANES) * step + meta[k * rows:(k + 1) * rows][None]
            grid_ref[k, pl.ds(b * (span // rows), span // rows)] = value
        return carry

    lax.fori_loop(0, blocks, decode, 0)
    group = 16

    def contact_group(i, carry):
        start = pl.multiple_of(i * group, group)
        for j in range(group):
            a = first_ref[start + j]
            b = second_ref[start + j]
            squared = None
            for k in range(3):
                offset = grid_ref[k, a] - grid_ref[k, b]
                term = offset * offset
                squared = term if squared is None else squared + term
            separation = jnp.sqrt(squared + 0.01)
            tmp[pl.ds(j, rows, stride=group), :] = 1.0 / (1.0 + jnp.exp((separation - 8.0) / 1.5))
        for s in range(rows):
            out_ref[pl.ds(start, group), s * LANES:(s + 1) * LANES] = (
                tmp[s * group:(s + 1) * group, :].astype(jnp.bfloat16)
            )
        return carry

    lax.fori_loop(0, contacts // group, contact_group, 0)


def featurize(first, second, codes, meta):
    blocks, _, span, _ = codes.shape
    rows = meta.shape[1] // 4
    contacts = first.shape[0]
    residues = blocks * span // rows
    whole = pl.BlockSpec(memory_space=pltpu.VMEM)
    scalars = pl.BlockSpec(memory_space=pltpu.SMEM)
    return pl.pallas_call(
        feature_kernel,
        in_specs=[scalars, scalars, whole, whole],
        out_specs=whole,
        out_shape=jax.ShapeDtypeStruct((contacts, rows * LANES), jnp.bfloat16),
        scratch_shapes=[
            pltpu.VMEM((3, residues, rows, LANES), jnp.float32),
            pltpu.VMEM((rows * 16, LANES), jnp.float32),
        ],
        compiler_params=pltpu.CompilerParams(vmem_limit_bytes=48 * 2**20),
    )(first, second, codes, meta)


PREV, SIDE, NEAR, FAR = range(4)


def exchange_kernel(blocks, chunks, own_ref, out_ref, own_t, visit, total, norms, own_norm, stage,
                    send_sem, recv_sem, out_sem):
    me = lax.axis_index("blocks")
    core = me % 2
    side = (me // 2) % 2
    ahead = (me + 4) % blocks
    behind = (me + blocks - 4) % blocks
    twin = me + 1 - 2 * core
    across = me + 2 - 4 * side
    contacts, frames = own_ref.shape
    depth = contacts // chunks

    barrier = pltpu.get_barrier_semaphore()
    for other in (ahead, behind, twin, across):
        pl.semaphore_signal(barrier, inc=1, device_id={"blocks": other}, device_id_type=MESH)
    pl.semaphore_wait(barrier, 4)

    def part(n):
        return pl.ds(pl.multiple_of(n * depth, depth), depth)

    def copy(stream, n, source, target):
        return pltpu.make_async_remote_copy(
            src_ref=source.at[part(n)],
            dst_ref=visit.at[stream, part(n)],
            send_sem=send_sem.at[stream, n],
            recv_sem=recv_sem.at[stream, n],
            device_id={"blocks": target},
            device_id_type=MESH,
        )

    prev = visit.at[PREV]

    def first_sends(n, carry):
        copy(PREV, n, own_ref, ahead).start()

        @pl.when(side == 0)
        def _():
            copy(SIDE, n, own_ref, across).start()

        @pl.when(core == 0)
        def _():
            copy(NEAR, n, own_ref, twin).start()

        return carry

    lax.fori_loop(0, chunks, first_sends, 0)

    norms[...] = jnp.zeros_like(norms)

    def turn(n, own):
        block = own_ref[part(n), :]
        own_t[n] = block.T
        wide = block.astype(jnp.float32)
        return own + jnp.sum(wide * wide, axis=0, keepdims=True)

    own = lax.fori_loop(0, chunks, turn, jnp.zeros((1, frames), jnp.float32))
    own_norm[...] = jnp.broadcast_to(own, (LANES, frames)).T

    tile = 256

    def add(stream, n):
        block = visit[stream, part(n), :]
        wide = block.astype(jnp.float32)
        norms[stream] += jnp.sum((wide * wide).reshape(depth // 8, 8, frames), axis=0)

        def rows_of(t, carry):
            at = pl.ds(pl.multiple_of(t * tile, tile), tile)
            product = jnp.dot(own_t[n, at, :], block_of(stream, n), preferred_element_type=jnp.float32)

            @pl.when(n == 0)
            def _():
                total[stream, at, :] = product

            @pl.when(n > 0)
            def _():
                total[stream, at, :] += product

            return carry

        lax.fori_loop(0, frames // tile, rows_of, 0)

    def block_of(stream, n):
        return visit[stream, part(n), :]

    def arrive(n, carry):
        @pl.when(n < chunks)
        def _():
            copy(PREV, n, own_ref, ahead).wait_recv()

            @pl.when(side == 1)
            def _():
                copy(SIDE, n, prev, across).start()

            @pl.when(core == 1)
            def _():
                copy(NEAR, n, prev, twin).start()

        @pl.when(n > 0)
        def _():
            copy(SIDE, n - 1, prev, across).wait_recv()
            copy(FAR, n - 1, visit.at[SIDE], twin).start()

        @pl.when(n < chunks)
        def _():
            add(PREV, n)

        @pl.when(n > 0)
        def _():
            copy(NEAR, n - 1, prev, twin).wait_recv()
            add(NEAR, n - 1)
            add(SIDE, n - 1)
            copy(FAR, n - 1, prev, twin).wait_recv()
            add(FAR, n - 1)

        return carry

    lax.fori_loop(0, chunks + 1, arrive, 0)

    def out_copy(stream, round_index):
        return pltpu.make_async_copy(stage.at[stream], out_ref.at[round_index], out_sem.at[stream])

    round_of = {PREV: 3, SIDE: 1, NEAR: 2 - 2 * core, FAR: 2 * core}
    for stream in (PREV, NEAR, SIDE, FAR):
        visiting = jnp.sum(norms[stream], axis=0, keepdims=True)

        def finish(t, carry):
            at = pl.ds(pl.multiple_of(t * tile, tile), tile)
            shared = total[stream, at, :]
            ratio = shared / (own_norm[at, :1] + visiting - shared + 1e-06)
            stage[stream, at, :] = (1.0 - ratio).astype(jnp.bfloat16)
            return carry

        lax.fori_loop(0, frames // tile, finish, 0)
        out_copy(stream, round_of[stream]).start()

    def drain(n, carry):
        for stream in range(4):
            copy(stream, n, prev, twin).wait_send()
        return carry

    lax.fori_loop(0, chunks, drain, 0)
    for stream in (PREV, NEAR, SIDE, FAR):
        out_copy(stream, round_of[stream]).wait()


def exchange(features, blocks):
    contacts, frames = features.shape
    chunks = 8
    depth = contacts // chunks
    return pl.pallas_call(
        functools.partial(exchange_kernel, blocks, chunks),
        in_specs=[pl.BlockSpec(memory_space=pltpu.VMEM)],
        out_specs=pl.BlockSpec(memory_space=pl.ANY),
        out_shape=jax.ShapeDtypeStruct((ROUNDS, frames, frames), jnp.bfloat16),
        scratch_shapes=[
            pltpu.VMEM((chunks, frames, depth), jnp.bfloat16),
            pltpu.VMEM((4, contacts, frames), jnp.bfloat16),
            pltpu.VMEM((4, frames, frames), jnp.float32),
            pltpu.VMEM((4, 8, frames), jnp.float32),
            pltpu.VMEM((frames, LANES), jnp.float32),
            pltpu.VMEM((4, frames, frames), jnp.bfloat16),
            pltpu.SemaphoreType.DMA((4, chunks)),
            pltpu.SemaphoreType.DMA((4, chunks)),
            pltpu.SemaphoreType.DMA((4,)),
        ],
        compiler_params=pltpu.CompilerParams(
            collective_id=1, has_side_effects=True, vmem_limit_bytes=60 * 2**20
        ),
    )(features)


def shards(coords, pairs, res_slot):
    blocks = lax.axis_size("blocks")
    residues = coords.shape[0] * blocks
    position = (
        jnp.zeros((residues,), jnp.int32).at[res_slot].set(jnp.arange(residues, dtype=jnp.int32))
    )
    codes, meta = encode(coords.transpose(1, 0, 2), blocks)
    codes = lax.all_to_all(codes, "blocks", 0, 0, tiled=True)
    meta = lax.all_to_all(meta, "blocks", 0, 0, tiled=True)
    features = featurize(position[pairs[0]], position[pairs[1]], codes, meta)
    return exchange(features, blocks)


def solution(mesh):
    in_specs = (P("blocks", None, "parts"), P(), P())
    out_specs = P(None, ("parts", "blocks"), None)
    return jax.shard_map(shards, mesh=mesh, in_specs=in_specs, out_specs=out_specs, check_vma=False)
```

```python
import functools
import math
import jax
import jax.numpy as jnp
from jax import lax
from jax.experimental import pallas as pl
from jax.experimental.pallas import tpu as pltpu
from jax.sharding import PartitionSpec as P

ROUNDS = 4
LANES = 128
TOP_CODE = 32000.0
COARSE = 256.0
LOG_TWO = math.log(2.0)
MESH = pl.DeviceIdType.MESH


def step_of(exponent):
    return jnp.exp(exponent * LOG_TWO)


def encode_kernel(x_ref, code_ref, tmp, params):
    _, res, frames = x_ref.shape
    rows = frames // LANES
    centers = []
    finest = jnp.full((1, frames), 1e-30, jnp.float32)
    for k in range(3):
        x = x_ref[k]
        top = jnp.max(x, axis=0, keepdims=True)
        low = jnp.min(x, axis=0, keepdims=True)
        center = 0.5 * top + 0.5 * low
        reach = jnp.maximum(top - center, center - low)
        finest = jnp.maximum(finest, jnp.maximum(reach, jnp.abs(center) * (1.0 / COARSE)) * (1.0 / TOP_CODE))
        centers.append(center)
    exponent = jnp.ceil(jnp.log(finest) * (1.0 / LOG_TWO))
    step = step_of(exponent)
    inverse = 1.0 / step
    planes = []
    for k in range(3):
        center_code = jnp.round(centers[k] * (1.0 / COARSE) * inverse)
        planes.append(center_code)
        scaled = jnp.round((x_ref[k] - center_code * (COARSE * step)) * inverse)
        for s in range(rows):
            tmp[pl.ds(s, res, stride=rows), :] = scaled[:, s * LANES:(s + 1) * LANES]
        code_ref[0, k * res * rows:(k + 1) * res * rows] = tmp[...].astype(jnp.int32).astype(jnp.int16)
    for k, plane in enumerate(planes + [exponent]):
        for s in range(rows):
            params[k * rows + s:k * rows + s + 1, :] = plane[:, s * LANES:(s + 1) * LANES]
    code_ref[0, 3 * res * rows:] = params[...].astype(jnp.int32).astype(jnp.int16)


def encode(coords, blocks):
    _, res, frames = coords.shape
    per_block = frames // blocks
    rows = per_block // LANES
    span = (3 * res + 4) * rows
    return pl.pallas_call(
        encode_kernel,
        grid=(blocks,),
        in_specs=[pl.BlockSpec((3, res, per_block), lambda d: (0, 0, d))],
        out_specs=pl.BlockSpec((1, span, LANES), lambda d: (d, 0, 0)),
        out_shape=jax.ShapeDtypeStruct((blocks, span, LANES), jnp.int16),
        scratch_shapes=[
            pltpu.VMEM((res * rows, LANES), jnp.float32),
            pltpu.VMEM((4 * rows, LANES), jnp.float32),
        ],
        compiler_params=pltpu.CompilerParams(vmem_limit_bytes=32 * 2**20),
    )(coords)


PREV, SIDE, NEAR, FAR = range(4)


def exchange_kernel(blocks, chunks, first_ref, second_ref, code_ref, out_ref, grid_ref, tmp, own_ref,
                    own_t, visit, total, norms, own_norm, stage, send_sem, recv_sem, out_sem):
    me = lax.axis_index("blocks")
    core = me % 2
    side = (me // 2) % 2
    ahead = (me + 4) % blocks
    behind = (me + blocks - 4) % blocks
    twin = me + 1 - 2 * core
    across = me + 2 - 4 * side
    contacts, frames = own_ref.shape
    rows = frames // LANES
    res = grid_ref.shape[1] // blocks
    depth = contacts // chunks
    wide_depth = 2 * depth

    barrier = pltpu.get_barrier_semaphore()
    for other in (ahead, behind, twin, across):
        pl.semaphore_signal(barrier, inc=1, device_id={"blocks": other}, device_id_type=MESH)

    def decode(b, carry):
        def numbers(start, count):
            return code_ref[b, start:start + count].astype(jnp.int32).astype(jnp.float32)

        params = numbers(3 * res * rows, 4 * rows)
        step = step_of(params[3 * rows:])
        for k in range(3):
            center = params[k * rows:(k + 1) * rows] * (COARSE * step)
            code = numbers(k * res * rows, res * rows).reshape(res, rows, LANES)
            grid_ref[k, pl.ds(b * res, res)] = code * step[None] + center[None]
        return carry

    lax.fori_loop(0, blocks, decode, 0)
    pl.semaphore_wait(barrier, 4)

    def part(n):
        return pl.ds(pl.multiple_of(n * depth, depth), depth)

    def pair(m):
        return pl.ds(pl.multiple_of(m * wide_depth, wide_depth), wide_depth)

    def copy(stream, n, source, target):
        return pltpu.make_async_remote_copy(
            src_ref=source.at[part(n)],
            dst_ref=visit.at[stream, part(n)],
            send_sem=send_sem.at[stream, n],
            recv_sem=recv_sem.at[stream, n],
            device_id={"blocks": target},
            device_id_type=MESH,
        )

    prev = visit.at[PREV]
    group = 16

    def features(n, carry):
        def contact_group(i, inner):
            start = pl.multiple_of(n * depth + i * group, group)
            for j in range(group):
                a = first_ref[start + j]
                b = second_ref[start + j]
                squared = None
                for k in range(3):
                    offset = grid_ref[k, a] - grid_ref[k, b]
                    term = offset * offset
                    squared = term if squared is None else squared + term
                separation = jnp.sqrt(squared + 0.01)
                tmp[pl.ds(j, rows, stride=group), :] = 1.0 / (1.0 + jnp.exp((separation - 8.0) / 1.5))
            for s in range(rows):
                own_ref[pl.ds(start, group), s * LANES:(s + 1) * LANES] = (
                    tmp[s * group:(s + 1) * group, :].astype(jnp.bfloat16)
                )
            return inner

        lax.fori_loop(0, depth // group, contact_group, 0)
        copy(PREV, n, own_ref, ahead).start()

        @pl.when(side == 0)
        def _():
            copy(SIDE, n, own_ref, across).start()

        @pl.when(core == 0)
        def _():
            copy(NEAR, n, own_ref, twin).start()

        return carry

    lax.fori_loop(0, chunks, features, 0)
    norms[...] = jnp.zeros_like(norms)
    tile = 256

    def squares(block):
        wide = block.astype(jnp.float32)
        return jnp.sum((wide * wide).reshape(wide_depth // 8, 8, frames), axis=0)

    def turn(m):
        block = own_ref[pair(m), :]
        own_t[m] = block.T
        norms[4] += squares(block)

    def add(stream, m):
        norms[stream] += squares(visit[stream, pair(m), :])

        def rows_of(t, carry):
            at = pl.ds(pl.multiple_of(t * tile, tile), tile)
            product = jnp.dot(
                own_t[m, at, :], visit[stream, pair(m), :], preferred_element_type=jnp.float32
            )

            @pl.when(m == 0)
            def _():
                total[stream, at, :] = product

            @pl.when(m > 0)
            def _():
                total[stream, at, :] += product

            return carry

        lax.fori_loop(0, frames // tile, rows_of, 0)

    def pass_far(n):
        copy(SIDE, n, prev, across).wait_recv()
        copy(FAR, n, visit.at[SIDE], twin).start()

    def arrive(n, carry):
        copy(PREV, n, own_ref, ahead).wait_recv()

        @pl.when(side == 1)
        def _():
            copy(SIDE, n, prev, across).start()

        @pl.when(core == 1)
        def _():
            copy(NEAR, n, prev, twin).start()

        @pl.when(n > 0)
        def _():
            pass_far(n - 1)

        m = n // 2

        @pl.when(n % 2 == 1)
        def _():
            turn(m)
            add(PREV, m)
            copy(NEAR, n - 1, prev, twin).wait_recv()
            copy(NEAR, n, prev, twin).wait_recv()
            add(NEAR, m)

        @pl.when((n % 2 == 0) & (n > 0))
        def _():
            add(SIDE, m - 1)
            copy(FAR, n - 2, prev, twin).wait_recv()
            copy(FAR, n - 1, prev, twin).wait_recv()
            add(FAR, m - 1)

        return carry

    lax.fori_loop(0, chunks, arrive, 0)

    slot_of = {PREV: 0, NEAR: 1, SIDE: 0, FAR: 1}
    round_of = {PREV: 3, SIDE: 1, NEAR: 2 - 2 * core, FAR: 2 * core}

    def out_copy(stream):
        return pltpu.make_async_copy(
            stage.at[slot_of[stream]], out_ref.at[round_of[stream]], out_sem.at[stream]
        )

    def finish(stream):
        visiting = jnp.sum(norms[stream], axis=0, keepdims=True)

        def rows_of(t, carry):
            at = pl.ds(pl.multiple_of(t * tile, tile), tile)
            shared = total[stream, at, :]
            ratio = shared / (own_norm[at, :1] + visiting - shared + 1e-06)
            stage[slot_of[stream], at, :] = (1.0 - ratio).astype(jnp.bfloat16)
            return carry

        lax.fori_loop(0, frames // tile, rows_of, 0)
        out_copy(stream).start()

    last = chunks // 2 - 1
    own = jnp.sum(norms[4], axis=0, keepdims=True)
    own_norm[...] = jnp.broadcast_to(own, (LANES, frames)).T
    finish(PREV)
    pass_far(chunks - 1)
    finish(NEAR)
    add(SIDE, last)
    out_copy(PREV).wait()
    finish(SIDE)
    copy(FAR, chunks - 2, prev, twin).wait_recv()
    copy(FAR, chunks - 1, prev, twin).wait_recv()
    add(FAR, last)
    out_copy(NEAR).wait()
    finish(FAR)

    def drain(n, carry):
        for stream in range(4):
            copy(stream, n, prev, twin).wait_send()
        return carry

    lax.fori_loop(0, chunks, drain, 0)
    out_copy(SIDE).wait()
    out_copy(FAR).wait()


def exchange(first, second, codes, residues):
    blocks, span, _ = codes.shape
    contacts = first.shape[0]
    rows = span // (3 * (residues // blocks) + 4)
    frames = rows * LANES
    chunks = 16
    depth = contacts // chunks
    scalars = pl.BlockSpec(memory_space=pltpu.SMEM)
    return pl.pallas_call(
        functools.partial(exchange_kernel, blocks, chunks),
        in_specs=[scalars, scalars, pl.BlockSpec(memory_space=pltpu.VMEM)],
        out_specs=pl.BlockSpec(memory_space=pl.ANY),
        out_shape=jax.ShapeDtypeStruct((ROUNDS, frames, frames), jnp.bfloat16),
        scratch_shapes=[
            pltpu.VMEM((3, residues, rows, LANES), jnp.float32),
            pltpu.VMEM((rows * 16, LANES), jnp.float32),
            pltpu.VMEM((contacts, frames), jnp.bfloat16),
            pltpu.VMEM((chunks // 2, frames, 2 * depth), jnp.bfloat16),
            pltpu.VMEM((4, contacts, frames), jnp.bfloat16),
            pltpu.VMEM((4, frames, frames), jnp.float32),
            pltpu.VMEM((5, 8, frames), jnp.float32),
            pltpu.VMEM((frames, LANES), jnp.float32),
            pltpu.VMEM((2, frames, frames), jnp.bfloat16),
            pltpu.SemaphoreType.DMA((4, chunks)),
            pltpu.SemaphoreType.DMA((4, chunks)),
            pltpu.SemaphoreType.DMA((4,)),
        ],
        compiler_params=pltpu.CompilerParams(
            collective_id=1, has_side_effects=True, vmem_limit_bytes=60 * 2**20
        ),
    )(first, second, codes)


def shards(coords, pairs, res_slot):
    blocks = lax.axis_size("blocks")
    residues = coords.shape[0] * blocks
    position = (
        jnp.zeros((residues,), jnp.int32).at[res_slot].set(jnp.arange(residues, dtype=jnp.int32))
    )
    codes = encode(coords.transpose(1, 0, 2), blocks)
    codes = lax.all_to_all(codes, "blocks", 0, 0, tiled=True)
    return exchange(position[pairs[0]], position[pairs[1]], codes, residues)


def solution(mesh):
    in_specs = (P("blocks", None, "parts"), P(), P())
    out_specs = P(None, ("parts", "blocks"), None)
    return jax.shard_map(shards, mesh=mesh, in_specs=in_specs, out_specs=out_specs, check_vma=False)
```

```python
import functools
import math
import jax
import jax.numpy as jnp
from jax import lax
from jax.experimental import pallas as pl
from jax.experimental.pallas import tpu as pltpu
from jax.sharding import PartitionSpec as P

ROUNDS = 4
LANES = 128
TOP_CODE = 32000.0
COARSE = 256.0
LOG_TWO = math.log(2.0)
MESH = pl.DeviceIdType.MESH


def step_of(exponent):
    return jnp.exp(exponent * LOG_TWO)


def encode_kernel(x_ref, code_ref, tmp, params):
    _, res, frames = x_ref.shape
    rows = frames // LANES
    centers = []
    finest = jnp.full((1, frames), 1e-30, jnp.float32)
    for k in range(3):
        x = x_ref[k]
        top = jnp.max(x, axis=0, keepdims=True)
        low = jnp.min(x, axis=0, keepdims=True)
        center = 0.5 * top + 0.5 * low
        reach = jnp.maximum(top - center, center - low)
        finest = jnp.maximum(finest, jnp.maximum(reach, jnp.abs(center) * (1.0 / COARSE)) * (1.0 / TOP_CODE))
        centers.append(center)
    exponent = jnp.ceil(jnp.log(finest) * (1.0 / LOG_TWO))
    step = step_of(exponent)
    inverse = 1.0 / step
    planes = []
    for k in range(3):
        center_code = jnp.round(centers[k] * (1.0 / COARSE) * inverse)
        planes.append(center_code)
        scaled = jnp.round((x_ref[k] - center_code * (COARSE * step)) * inverse)
        for s in range(rows):
            tmp[pl.ds(s, res, stride=rows), :] = scaled[:, s * LANES:(s + 1) * LANES]
        code_ref[0, k * res * rows:(k + 1) * res * rows] = tmp[...].astype(jnp.int32).astype(jnp.int16)
    for k, plane in enumerate(planes + [exponent]):
        for s in range(rows):
            params[k * rows + s:k * rows + s + 1, :] = plane[:, s * LANES:(s + 1) * LANES]
    code_ref[0, 3 * res * rows:] = params[...].astype(jnp.int32).astype(jnp.int16)


def encode(coords, blocks):
    _, res, frames = coords.shape
    per_block = frames // blocks
    rows = per_block // LANES
    span = (3 * res + 4) * rows
    return pl.pallas_call(
        encode_kernel,
        grid=(blocks,),
        in_specs=[pl.BlockSpec((3, res, per_block), lambda d: (0, 0, d))],
        out_specs=pl.BlockSpec((1, span, LANES), lambda d: (d, 0, 0)),
        out_shape=jax.ShapeDtypeStruct((blocks, span, LANES), jnp.int16),
        scratch_shapes=[
            pltpu.VMEM((res * rows, LANES), jnp.float32),
            pltpu.VMEM((4 * rows, LANES), jnp.float32),
        ],
        compiler_params=pltpu.CompilerParams(vmem_limit_bytes=56 * 2**20),
    )(coords)


PREV, SIDE, NEAR, FAR = range(4)


def exchange_kernel(blocks, chunks, first_ref, second_ref, code_ref, out_ref, vis_out, own_out, grid_ref, tmp,
                    own_ref, own_t, visit, total, norms, own_norm, send_sem, recv_sem, out_sem):
    me = lax.axis_index("blocks")
    core = me % 2
    side = (me // 2) % 2
    ahead = (me + 4) % blocks
    behind = (me + blocks - 4) % blocks
    twin = me + 1 - 2 * core
    across = me + 2 - 4 * side
    contacts, frames = own_ref.shape
    rows = frames // LANES
    res = grid_ref.shape[1] // blocks
    depth = contacts // chunks
    wide_depth = 2 * depth

    barrier = pltpu.get_barrier_semaphore()
    for other in (ahead, behind, twin, across):
        pl.semaphore_signal(barrier, inc=1, device_id={"blocks": other}, device_id_type=MESH)

    def decode(b, carry):
        def numbers(start, count):
            return code_ref[b, start:start + count].astype(jnp.int32).astype(jnp.float32)

        params = numbers(3 * res * rows, 4 * rows)
        step = step_of(params[3 * rows:])
        for k in range(3):
            center = params[k * rows:(k + 1) * rows] * (COARSE * step)
            code = numbers(k * res * rows, res * rows).reshape(res, rows, LANES)
            grid_ref[k, pl.ds(b * res, res)] = code * step[None] + center[None]
        return carry

    lax.fori_loop(0, blocks, decode, 0)
    pl.semaphore_wait(barrier, 4)

    def part(n):
        return pl.ds(pl.multiple_of(n * depth, depth), depth)

    def pair(m):
        return pl.ds(pl.multiple_of(m * wide_depth, wide_depth), wide_depth)

    def copy(stream, n, source, target):
        return pltpu.make_async_remote_copy(
            src_ref=source.at[part(n)],
            dst_ref=visit.at[stream, part(n)],
            send_sem=send_sem.at[stream, n],
            recv_sem=recv_sem.at[stream, n],
            device_id={"blocks": target},
            device_id_type=MESH,
        )

    prev = visit.at[PREV]
    group = 16

    def features(n, carry):
        def contact_group(i, inner):
            start = pl.multiple_of(n * depth + i * group, group)
            for j in range(group):
                a = first_ref[start + j]
                b = second_ref[start + j]
                squared = None
                for k in range(3):
                    offset = grid_ref[k, a] - grid_ref[k, b]
                    term = offset * offset
                    squared = term if squared is None else squared + term
                separation = jnp.sqrt(squared + 0.01)
                tmp[pl.ds(j, rows, stride=group), :] = 1.0 / (1.0 + jnp.exp((separation - 8.0) / 1.5))
            for s in range(rows):
                own_ref[pl.ds(start, group), s * LANES:(s + 1) * LANES] = (
                    tmp[s * group:(s + 1) * group, :].astype(jnp.bfloat16)
                )
            return inner

        lax.fori_loop(0, depth // group, contact_group, 0)
        copy(PREV, n, own_ref, ahead).start()

        @pl.when(side == 0)
        def _():
            copy(SIDE, n, own_ref, across).start()

        @pl.when(core == 0)
        def _():
            copy(NEAR, n, own_ref, twin).start()

        return carry

    lax.fori_loop(0, chunks, features, 0)
    norms[...] = jnp.zeros_like(norms)
    tile = 256

    def squares(block):
        wide = block.astype(jnp.float32)
        return jnp.sum((wide * wide).reshape(wide_depth // 8, 8, frames), axis=0)

    def turn(m):
        block = own_ref[pair(m), :]
        own_t[m] = block.T
        norms[4] += squares(block)

    def add(stream, m):
        norms[stream] += squares(visit[stream, pair(m), :])

        def rows_of(t, carry):
            at = pl.ds(pl.multiple_of(t * tile, tile), tile)
            product = jnp.dot(
                own_t[m, at, :], visit[stream, pair(m), :], preferred_element_type=jnp.float32
            )

            @pl.when(m == 0)
            def _():
                total[stream, at, :] = product

            @pl.when(m > 0)
            def _():
                total[stream, at, :] += product

            return carry

        lax.fori_loop(0, frames // tile, rows_of, 0)

    def pass_far(n):
        copy(SIDE, n, prev, across).wait_recv()
        copy(FAR, n, visit.at[SIDE], twin).start()

    def arrive(n, carry):
        copy(PREV, n, own_ref, ahead).wait_recv()

        @pl.when(side == 1)
        def _():
            copy(SIDE, n, prev, across).start()

        @pl.when(core == 1)
        def _():
            copy(NEAR, n, prev, twin).start()

        @pl.when(n > 0)
        def _():
            pass_far(n - 1)

        m = n // 2

        @pl.when(n % 2 == 1)
        def _():
            turn(m)
            add(PREV, m)
            copy(NEAR, n - 1, prev, twin).wait_recv()
            copy(NEAR, n, prev, twin).wait_recv()
            add(NEAR, m)

        @pl.when((n % 2 == 0) & (n > 0))
        def _():
            add(SIDE, m - 1)
            copy(FAR, n - 2, prev, twin).wait_recv()
            copy(FAR, n - 1, prev, twin).wait_recv()
            add(FAR, m - 1)

        return carry

    lax.fori_loop(0, chunks, arrive, 0)

    round_of = {PREV: 3, SIDE: 1, NEAR: 2 - 2 * core, FAR: 2 * core}

    def out_copies(stream):
        at = round_of[stream]
        return (
            pltpu.make_async_copy(total.at[stream], out_ref.at[at], out_sem.at[2 * stream]),
            pltpu.make_async_copy(norms.at[stream], vis_out.at[at], out_sem.at[2 * stream + 1]),
        )

    def finish(stream):
        for each in out_copies(stream):
            each.start()

    last = chunks // 2 - 1
    finish(PREV)
    finish(NEAR)
    own = jnp.sum(norms[4], axis=0, keepdims=True)
    own_norm[...] = jnp.broadcast_to(own, (LANES, frames)).T
    own_copy = pltpu.make_async_copy(own_norm, own_out, out_sem.at[8])
    own_copy.start()
    pass_far(chunks - 1)
    add(SIDE, last)
    finish(SIDE)
    copy(FAR, chunks - 2, prev, twin).wait_recv()
    copy(FAR, chunks - 1, prev, twin).wait_recv()
    add(FAR, last)
    finish(FAR)

    def drain(n, carry):
        for stream in range(4):
            copy(stream, n, prev, twin).wait_send()
        return carry

    lax.fori_loop(0, chunks, drain, 0)
    own_copy.wait()
    for stream in (PREV, NEAR, SIDE, FAR):
        for each in out_copies(stream):
            each.wait()


def exchange(first, second, codes, residues):
    blocks, span, _ = codes.shape
    contacts = first.shape[0]
    rows = span // (3 * (residues // blocks) + 4)
    frames = rows * LANES
    chunks = 16
    depth = contacts // chunks
    scalars = pl.BlockSpec(memory_space=pltpu.SMEM)
    return pl.pallas_call(
        functools.partial(exchange_kernel, blocks, chunks),
        in_specs=[scalars, scalars, pl.BlockSpec(memory_space=pltpu.VMEM)],
        out_specs=[pl.BlockSpec(memory_space=pl.ANY)] * 3,
        out_shape=[
            jax.ShapeDtypeStruct((ROUNDS, frames, frames), jnp.float32),
            jax.ShapeDtypeStruct((ROUNDS, 8, frames), jnp.float32),
            jax.ShapeDtypeStruct((frames, LANES), jnp.float32),
        ],
        scratch_shapes=[
            pltpu.VMEM((3, residues, rows, LANES), jnp.float32),
            pltpu.VMEM((rows * 16, LANES), jnp.float32),
            pltpu.VMEM((contacts, frames), jnp.bfloat16),
            pltpu.VMEM((chunks // 2, frames, 2 * depth), jnp.bfloat16),
            pltpu.VMEM((4, contacts, frames), jnp.bfloat16),
            pltpu.VMEM((4, frames, frames), jnp.float32),
            pltpu.VMEM((5, 8, frames), jnp.float32),
            pltpu.VMEM((frames, LANES), jnp.float32),
            pltpu.SemaphoreType.DMA((4, chunks)),
            pltpu.SemaphoreType.DMA((4, chunks)),
            pltpu.SemaphoreType.DMA((9,)),
        ],
        compiler_params=pltpu.CompilerParams(
            collective_id=1, has_side_effects=True, vmem_limit_bytes=60 * 2**20
        ),
    )(first, second, codes)


def distance_kernel(shared_ref, visiting_ref, own_ref, out_ref):
    visiting = jnp.sum(visiting_ref[0], axis=0, keepdims=True)
    shared = shared_ref[0]
    ratio = shared / (own_ref[:, :1] + visiting - shared + 1e-06)
    out_ref[0] = (1.0 - ratio).astype(jnp.bfloat16)


def distances_of(shared, visiting, own):
    rounds, frames, _ = shared.shape
    tile = min(256, frames)
    block = pl.BlockSpec((1, tile, frames), lambda r, t: (r, t, 0))
    return pl.pallas_call(
        distance_kernel,
        grid=(rounds, frames // tile),
        in_specs=[
            block,
            pl.BlockSpec((1, 8, frames), lambda r, t: (r, 0, 0)),
            pl.BlockSpec((tile, LANES), lambda r, t: (t, 0)),
        ],
        out_specs=block,
        out_shape=jax.ShapeDtypeStruct(shared.shape, jnp.bfloat16),
        compiler_params=pltpu.CompilerParams(vmem_limit_bytes=56 * 2**20),
    )(shared, visiting, own)


def shards(coords, pairs, res_slot):
    blocks = lax.axis_size("blocks")
    residues = coords.shape[0] * blocks
    position = (
        jnp.zeros((residues,), jnp.int32).at[res_slot].set(jnp.arange(residues, dtype=jnp.int32))
    )
    codes = encode(coords.transpose(1, 0, 2), blocks)
    codes = lax.all_to_all(codes, "blocks", 0, 0, tiled=True)
    return distances_of(*exchange(position[pairs[0]], position[pairs[1]], codes, residues))


def solution(mesh):
    in_specs = (P("blocks", None, "parts"), P(), P())
    out_specs = P(None, ("parts", "blocks"), None)
    return jax.shard_map(shards, mesh=mesh, in_specs=in_specs, out_specs=out_specs, check_vma=False)
```
